32 devices in a mesh: dp: 4 (over x, core), term: 8 (over z, y).
Axes of the slice: x: 2, y: 2, z: 4, core: 2. Of those that a mesh axis runs over, the one named last changes fastest.
Arguments:
- inputs: bfloat16 [1024, 8192], P('dp'), may hold values from -6 to 6
- cotangent: bfloat16 [1024, 8192], P('dp', 'term'), may hold values from -6 to 6
- logits: float32 [1024, 256], P('dp'), may hold values from -20 to 320
- in_factor: bfloat16 [8192, 2048], P(None, 'term'), may hold values from -0.09375 to 0.09375
- out_factor: bfloat16 [8192, 2048], P(None, 'term'), may hold values from -0.0625 to 0.0625
- expert_factor: bfloat16 [256, 2048], P(None, 'term'), may hold values from -3 to 3
Outputs:
- grad_inputs: bfloat16 [1024, 8192], P('dp', 'term')
- grad_logits: float32 [1024, 256], P('dp', 'term')
- grad_in_factor: float32 [8192, 2048], P('dp', 'term')
- grad_out_factor: float32 [8192, 2048], P('dp', 'term')
- grad_expert_factor: float32 [256, 2048], P('dp', 'term')
The draws below stay inside these ranges and needn't reach their ends.
All inputs are finite; a program needn't handle non-finite values.
Results may differ from the reference program's by a relative error of at most 0.028.
Values may be sent and summed in bfloat16 or wider, within the bound.
A program may use at most 128 MiB of HBM per device.

```python
import math
import jax
import jax.numpy as jnp
from jax import lax

D = 8192
E = 256
R = 2048
TOK_DEV = 256
TOKENS = 1024
N_DP = 4
N_TERM = 8


def draw_logits(key, part):
    base = jnp.clip(jax.random.normal(key, (TOKENS, E), jnp.float32) * 3.0, -15.0, 15.0)
    return base


def strengthened(drawn, rng, source, target, shards_of, factor):
    def block_of(position):
        return (jnp.arange(drawn.shape[position]) // (drawn.shape[position] // shards_of)).reshape((-1,) + (1,) * (drawn.ndim - 1 - position))

    one_side = jax.random.permutation(rng, shards_of)[block_of(target)]
    far = (block_of(target) + shards_of // 2) % shards_of
    return jnp.where((block_of(source) == one_side) | (block_of(source) == far), factor * drawn, drawn)


def block_scale(stream_key, dims, shards, smallest, top_value):
    gain, own = 1.0, jax.random.fold_in(stream_key, 6)
    for dim, parts in shards:
        draws = jnp.exp(jax.random.uniform(jax.random.fold_in(own, dim), (parts,), jnp.float32, smallest / len(shards), top_value / len(shards)))
        gain = gain * jnp.repeat(draws, dims[dim] // parts).reshape([-1 if axis == dim else 1 for axis in range(len(dims))])
    return gain


def noise(key, extent, deviation, reach, shards=(), kind=jnp.bfloat16):
    array = jax.random.normal(key, extent, jnp.float32) * deviation
    if len(shards) > 0:
        array = block_scale(key, extent, shards, -0.22, 0.18) * array
    return jnp.clip(array, min=-reach, max=reach).astype(kind)


def noise_with(own_key, extent, spread, most, pieces, heavy, held_as=jnp.bfloat16):
    result = spread * jax.random.normal(own_key, extent, jnp.float32)
    if pieces:
        result = result * block_scale(own_key, extent, pieces, -0.22, 0.18)
    return jnp.clip(strengthened(result, jax.random.fold_in(own_key, 3), *heavy), -most, most).astype(held_as)


def setup_inputs(seed: int = 0) -> dict:
    splits = jax.random.split(jax.random.key(seed), 7)
    return {
        "inputs": noise_with(splits[0], (TOKENS, D), 1.0, 6.0, ((0, 4),), (0, 1, 4, 2.0)),
        "cotangent": noise_with(splits[1], (TOKENS, D), 1.0, 6.0, ((0, 4), (1, 8)), (0, 1, 8, 2.0)),
        "logits": draw_logits(jax.random.fold_in(splits[6], 71), 0),
        "in_factor": noise_with(splits[3], (D, R), D ** -0.5, 0.09375, ((1, 8),), (1, 0, 8, 2.0)),
        "out_factor": noise(splits[4], (D, R), D ** -0.5, 0.0625, ((1, 8),)),
        "expert_factor": noise(splits[5], (E, R), 0.5, 3.0, ((1, 8),)),
    }


def rounded(value):
    return lax.optimization_barrier(value.astype(jnp.bfloat16)).astype(jnp.float32)

def reference(inputs, cotangent, logits, in_factor, out_factor, expert_factor):
    fl = jnp.float32
    gates = jax.nn.softmax(logits, axis=-1)
    gates_bf = gates.astype(jnp.bfloat16)
    inputs_f = inputs.astype(fl)
    cotan_f = cotangent.astype(fl)
    in_f = in_factor.astype(fl)
    out_f = out_factor.astype(fl)
    exp_f = expert_factor.astype(fl)
    proj_in = jnp.dot(inputs_f, in_f)
    proj_exp = jnp.dot(gates_bf.astype(fl), exp_f)
    hidden = (proj_in * proj_exp).astype(jnp.bfloat16)
    grad_hid = jnp.dot(cotan_f, out_f)
    grad_pin = (grad_hid * proj_exp).astype(jnp.bfloat16)
    grad_pexp = (grad_hid * proj_in).astype(jnp.bfloat16)
    row_total = lax.optimization_barrier(jnp.sum(grad_hid * proj_in * proj_exp, axis=1, keepdims=True))
    width = R // N_TERM
    pin_f = grad_pin.astype(fl)
    pexp_f = grad_pexp.astype(fl)

    def term_block(carry, index):
        start = (index * width).astype(jnp.int32)
        pin_blk = lax.dynamic_slice_in_dim(pin_f, start, width, 1)
        pexp_blk = lax.dynamic_slice_in_dim(pexp_f, start, width, 1)
        in_blk = lax.dynamic_slice_in_dim(in_f, start, width, 1)
        exp_blk = lax.dynamic_slice_in_dim(exp_f, start, width, 1)
        part_x = rounded(jnp.dot(pin_blk, in_blk.T))
        part_g = rounded(jnp.dot(pexp_blk, exp_blk.T))
        return ((carry[0] + part_x, carry[1] + part_g), None)
    init = (jnp.zeros((TOKENS, D), fl), jnp.zeros((TOKENS, E), fl))
    (sum_x, grad_gate), _ = lax.scan(term_block, init, jnp.arange(N_TERM, dtype=jnp.int32))
    grad_inputs = sum_x.astype(jnp.bfloat16)
    grad_logits = gates * (grad_gate - row_total)
    scale = 1.0 / math.sqrt(TOKENS)
    hid_f = hidden.astype(fl)
    gbf = gates_bf.astype(fl)

    def token_block(carry, index):
        start = (index * TOK_DEV).astype(jnp.int32)
        x_blk = lax.dynamic_slice_in_dim(inputs_f, start, TOK_DEV, 0)
        dy_blk = lax.dynamic_slice_in_dim(cotan_f, start, TOK_DEV, 0)
        g_blk = lax.dynamic_slice_in_dim(gbf, start, TOK_DEV, 0)
        pin_blk = lax.dynamic_slice_in_dim(pin_f, start, TOK_DEV, 0)
        pexp_blk = lax.dynamic_slice_in_dim(pexp_f, start, TOK_DEV, 0)
        hid_blk = lax.dynamic_slice_in_dim(hid_f, start, TOK_DEV, 0)
        part_i = rounded(jnp.dot(x_blk.T, pin_blk) * scale)
        part_o = rounded(jnp.dot(dy_blk.T, hid_blk) * scale)
        part_e = rounded(jnp.dot(g_blk.T, pexp_blk) * scale)
        return ((carry[0] + part_i, carry[1] + part_o, carry[2] + part_e), None)
    init2 = (jnp.zeros((D, R), fl), jnp.zeros((D, R), fl), jnp.zeros((E, R), fl))
    (grad_in, grad_out, grad_exp), _ = lax.scan(token_block, init2, jnp.arange(N_DP, dtype=jnp.int32))
    return (grad_inputs, grad_logits, grad_in, grad_out, grad_exp)
```

```python
import functools
import math

import jax
import jax.numpy as jnp
from jax import lax
from jax.experimental import pallas as pl
from jax.experimental.pallas import tpu as pltpu
from jax.sharding import PartitionSpec as P

FL = jnp.float32
BF = jnp.bfloat16
LAST = (((1,), (1,)), ((), ()))
FIRST = (((0,), (0,)), ((), ()))
SUBS = 2


def fused_kernel(
    n, m, scale,
    x_hbm, cot_ref, log_ref, fin_hbm, fout_hbm, fexp_ref,
    gx_ref, gl_ref, gin_ref, gout_ref, gexp_ref,
    x, fin, fout, cot, pin, pexp, ghid, hid, gpin, gpexp, gt, gbf,
    rs_send, rs_recv, c_send, c_recv, x_send, x_recv,
    g_send, g_recv, r_send, r_recv, e_send, e_recv,
    load_sem, ag_s, ag_r, rs_s, rs_r, c_s, c_r, xs_s, xs_r, g_s, g_r, r_s, r_r, e_s, e_r,
):
    t = lax.axis_index("term")
    a = lax.axis_index("dp")
    tok = cot_ref.shape[0]
    half = cot_ref.shape[1] // 2
    rows = tok // SUBS
    loads = [
        pltpu.make_async_copy(src, dst, load_sem.at[i])
        for i, (src, dst) in enumerate(((x_hbm, x), (fin_hbm, fin), (fout_hbm, fout)))
    ]
    for c in loads:
        c.start()
    barrier = pltpu.get_barrier_semaphore()
    for d in range(1, n):
        pl.semaphore_signal(barrier, inc=1, device_id={"term": lax.rem(t + d, n)}, device_id_type=pl.DeviceIdType.MESH)
    for d in range(1, m):
        pl.semaphore_signal(barrier, inc=1, device_id={"dp": lax.rem(a + d, m)}, device_id_type=pl.DeviceIdType.MESH)
    cot[t, 0] = cot_ref[:, :half]
    cot[t, 1] = cot_ref[:, half:]

    hz = n // 2
    pos = t // 2 + lax.rem(t, 2) * (n - 1 - 2 * (t // 2))

    def term_at(p):
        p = lax.rem(p + 2 * n, n)
        u = p // hz
        return (1 - u) * 2 * p + u * (2 * (n - 1 - p) + 1)

    ahead = (term_at(pos + 1), term_at(pos - 1))
    sign = (1, -1)
    streams = [(d, s) for d in range(2) for s in range(SUBS)]

    def remote(src, dst, ss, rs, dev):
        return pltpu.make_async_remote_copy(
            src_ref=src, dst_ref=dst, send_sem=ss, recv_sem=rs,
            device_id=dev, device_id_type=pl.DeviceIdType.MESH,
        )

    def ag(d, s, k, owner):
        ref = cot.at[owner, d, pl.ds(s * rows, rows), :]
        return remote(ref, ref, ag_s.at[d * SUBS + s, k], ag_r.at[d * SUBS + s, k], {"term": ahead[d]})

    pl.semaphore_wait(barrier, n + m - 2)
    for d, s in streams:
        ag(d, s, 0, t).start()

    z = log_ref[...]
    z = jnp.exp(z - jnp.max(z, axis=1, keepdims=True))
    gates = z / jnp.sum(z, axis=1, keepdims=True)
    gt[...] = jnp.transpose(gates)
    gbf[...] = gates.astype(BF)
    pexp[...] = jnp.dot(gbf[...], fexp_ref[...], preferred_element_type=FL)
    loads[0].wait()
    loads[1].wait()
    loads[2].wait()
    pin[...] = jnp.zeros_like(pin)
    wide = 2 * half

    @pl.loop(0, n)
    def _(i):
        at = pl.ds(pl.multiple_of(i * wide, wide), wide)
        pin[...] += jnp.dot(x[:, at], fin[at, :], preferred_element_type=FL)

    hid[...] = (pin[...] * pexp[...]).astype(BF)
    ghid[...] = jnp.zeros_like(ghid)

    def add_hid(d, owner):
        at = pl.ds(pl.multiple_of(owner * wide + d * half, half), half)
        ghid[...] += jnp.dot(cot[owner, d], fout[at, :], preferred_element_type=FL)

    add_hid(0, t)
    add_hid(1, t)

    @pl.loop(1, n)
    def _(k):
        for d, s in streams:
            owner = term_at(pos - sign[d] * k)
            ag(d, s, k - 1, owner).wait_recv()

            @pl.when(k < n - 1)
            def _():
                ag(d, s, k, owner).start()

        for d in range(2):
            add_hid(d, term_at(pos - sign[d] * k))

    gh = ghid[...]
    gpin[...] = (gh * pexp[...]).astype(BF)
    ghp = gh * pin[...]
    gpexp[...] = ghp.astype(BF)

    def part_x(d, s, owner):
        at = pl.ds(pl.multiple_of(owner * wide + d * half, half), half)
        return lax.dot_general(gpin[s * rows:(s + 1) * rows, :], fin[at, :], LAST, preferred_element_type=FL)

    def rs(d, s, k):
        i = d * SUBS + s
        return remote(rs_send.at[i, k], rs_recv.at[i, k], rs_s.at[i, k], rs_r.at[i, k], {"term": ahead[d]})

    for d, s in streams:
        rs_send[d * SUBS + s, 0] = part_x(d, s, term_at(pos - sign[d])).astype(BF)
        rs(d, s, 0).start()

    def rs_step(k):
        for d, s in streams:
            i = d * SUBS + s
            own = part_x(d, s, term_at(pos - sign[d] * (k + 1)))
            rs(d, s, k - 1).wait_recv()
            rs_send[i, k] = (own + rs_recv[i, k - 1].astype(FL)).astype(BF)
            rs(d, s, k).start()

    core = lax.rem(a, 2)
    xx = a // 2
    mate = {"dp": 2 * xx + 1 - core}
    across = {"dp": lax.rem(a + 2, m)}
    per = gin_ref.shape[0]
    cuts = per // half

    def part_f(w, owner, j):
        if w == 0:
            at = owner * (n // m) + j // 2
            lhs, rhs = cot[at, lax.rem(j, 2)], hid[...]
        else:
            lhs, rhs = x[:, pl.ds(pl.multiple_of(owner * per + j * half, half), half)], gpin[...]
        return lax.dot_general(lhs, rhs, FIRST, preferred_element_type=FL) * scale

    def to_mate(w, q, j):
        i = w * cuts + j
        return remote(c_send.at[q, i], c_recv.at[q, i], c_s.at[q, i], c_r.at[q, i], mate)

    def to_x(w, j):
        i = w * cuts + j
        return remote(x_send.at[i], x_recv.at[i], xs_s.at[i], xs_r.at[i], across)

    def give(w, q, chip):
        @pl.loop(0, cuts)
        def _(j):
            c_send[q, w * cuts + j] = part_f(w, 2 * chip + 1 - core, j).astype(BF)
            to_mate(w, q, j).start()

    def pass_on(w):
        @pl.loop(0, cuts)
        def _(j):
            own = part_f(w, 2 * (1 - xx) + core, j)
            to_mate(w, 0, j).wait_recv()
            x_send[w * cuts + j] = (own + c_recv[0, w * cuts + j].astype(FL)).astype(BF)
            to_x(w, j).start()

    outs = (gout_ref, gin_ref)

    def keep(w):
        @pl.loop(0, cuts)
        def _(j):
            own = part_f(w, a, j)
            to_mate(w, 1, j).wait_recv()
            at = pl.ds(pl.multiple_of(j * half, half), half)
            outs[w][at, :] = own + c_recv[1, w * cuts + j].astype(FL)

    def finish(w):
        @pl.loop(0, cuts)
        def _(j):
            to_x(w, j).wait_recv()
            at = pl.ds(pl.multiple_of(j * half, half), half)
            outs[w][at, :] += x_recv[w * cuts + j].astype(FL)

    give(0, 0, 1 - xx)
    pass_on(0)
    rs_step(1)
    give(1, 0, 1 - xx)
    pass_on(1)
    rs_step(2)

    share = gt.shape[0] // n
    row = jnp.sum(ghp * pexp[...], axis=1, keepdims=True)
    r_send[...] = jnp.transpose(jnp.broadcast_to(row, (tok, 128)))[:8]
    g_send[...] = lax.dot_general(fexp_ref[...], gpexp[...], LAST, preferred_element_type=FL).astype(BF)
    e_send[...] = (lax.dot_general(gbf[...], gpexp[...], FIRST, preferred_element_type=FL) * scale).astype(BF)
    eper = gexp_ref.shape[0]

    def g_copy(d):
        to = lax.rem(t + d, n)
        src = g_send.at[pl.ds(pl.multiple_of(to * share, share), share), :]
        return remote(src, g_recv.at[d - 1], g_s.at[d - 1], g_r.at[d - 1], {"term": to})

    def r_copy(d):
        return remote(r_send, r_recv.at[d - 1], r_s.at[d - 1], r_r.at[d - 1], {"term": lax.rem(t + d, n)})

    def e_copy(d):
        to = lax.rem(a + d, m)
        src = e_send.at[pl.ds(pl.multiple_of(to * eper, eper), eper), :]
        return remote(src, e_recv.at[d - 1], e_s.at[d - 1], e_r.at[d - 1], {"dp": to})

    for d in range(1, n):
        g_copy(d).start()
        r_copy(d).start()
    for d in range(1, m):
        e_copy(d).start()

    rs_step(3)
    give(0, 1, xx)
    give(1, 1, xx)
    rs_step(4)
    keep(0)
    keep(1)
    rs_step(5)
    mine = pl.ds(pl.multiple_of(t * share, share), share)
    gsum = g_send[mine, :].astype(FL)
    rsum = r_send[...]
    for d in range(1, n):
        g_copy(d).wait_recv()
        r_copy(d).wait_recv()
        gsum += g_recv[d - 1].astype(FL)
        rsum += r_recv[d - 1]
    gl_ref[...] = gt[mine, :] * (gsum - rsum[:1])
    esum = e_send[pl.ds(pl.multiple_of(a * eper, eper), eper), :].astype(FL)
    for d in range(1, m):
        e_copy(d).wait_recv()
        esum += e_recv[d - 1].astype(FL)
    gexp_ref[...] = esum
    for k in range(6, n - 1):
        rs_step(k)
    finish(0)
    finish(1)
    for d, s in streams:
        i = d * SUBS + s
        own = part_x(d, s, t)
        rs(d, s, n - 2).wait_recv()
        gx_ref[s * rows:(s + 1) * rows, d * half:(d + 1) * half] = (own + rs_recv[i, n - 2].astype(FL)).astype(BF)

    @pl.loop(0, n - 1)
    def _(k):
        for d, s in streams:
            ag(d, s, k, term_at(pos - sign[d] * k)).wait_send()
            rs(d, s, k).wait_send()

    for w in range(2):
        @pl.loop(0, cuts)
        def _(j):
            to_mate(w, 0, j).wait_send()
            to_mate(w, 1, j).wait_send()
            to_x(w, j).wait_send()

    for d in range(1, n):
        g_copy(d).wait_send()
        r_copy(d).wait_send()
    for d in range(1, m):
        e_copy(d).wait_send()


def fused(inputs, cotangent, logits, in_factor, out_factor, expert_factor):
    n, m = lax.axis_size("term"), lax.axis_size("dp")
    tok, wide = cotangent.shape
    width, rank = in_factor.shape
    experts = logits.shape[1]
    half, rows, per = wide // 2, tok // SUBS, width // m
    cuts = per // half
    ns = 2 * SUBS
    scale = 1.0 / math.sqrt(tok * m)
    shape = jax.ShapeDtypeStruct
    vm = pl.BlockSpec(memory_space=pltpu.VMEM)
    hbm = pl.BlockSpec(memory_space=pl.ANY)
    dma = pltpu.SemaphoreType.DMA
    out = pl.pallas_call(
        functools.partial(fused_kernel, n, m, scale),
        out_shape=(
            shape((tok, wide), BF),
            shape((experts // n, tok), FL),
            shape((per, rank), FL),
            shape((per, rank), FL),
            shape((experts // m, rank), FL),
        ),
        in_specs=[hbm, vm, vm, hbm, hbm, vm],
        out_specs=(vm,) * 5,
        scratch_shapes=[
            pltpu.VMEM((tok, width), BF),
            pltpu.VMEM((width, rank), BF),
            pltpu.VMEM((width, rank), BF),
            pltpu.VMEM((n, 2, tok, half), BF),
            pltpu.VMEM((tok, rank), FL),
            pltpu.VMEM((tok, rank), FL),
            pltpu.VMEM((tok, rank), FL),
            pltpu.VMEM((tok, rank), BF),
            pltpu.VMEM((tok, rank), BF),
            pltpu.VMEM((tok, rank), BF),
            pltpu.VMEM((experts, tok), FL),
            pltpu.VMEM((tok, experts), BF),
            pltpu.VMEM((ns, n - 1, rows, half), BF),
            pltpu.VMEM((ns, n - 1, rows, half), BF),
            pltpu.VMEM((2, 2 * cuts, half, rank), BF),
            pltpu.VMEM((2, 2 * cuts, half, rank), BF),
            pltpu.VMEM((2 * cuts, half, rank), BF),
            pltpu.VMEM((2 * cuts, half, rank), BF),
            pltpu.VMEM((experts, tok), BF),
            pltpu.VMEM((n - 1, experts // n, tok), BF),
            pltpu.VMEM((8, tok), FL),
            pltpu.VMEM((n - 1, 8, tok), FL),
            pltpu.VMEM((experts, rank), BF),
            pltpu.VMEM((m - 1, experts // m, rank), BF),
            dma((3,)),
            dma((ns, n - 1)), dma((ns, n - 1)), dma((ns, n - 1)), dma((ns, n - 1)),
            dma((2, 2 * cuts)), dma((2, 2 * cuts)), dma((2 * cuts,)), dma((2 * cuts,)),
            dma((n - 1,)), dma((n - 1,)), dma((n - 1,)), dma((n - 1,)),
            dma((m - 1,)), dma((m - 1,)),
        ],
        compiler_params=pltpu.CompilerParams(
            collective_id=0, has_side_effects=True, vmem_limit_bytes=60 * 2**20
        ),
        cost_estimate=pl.CostEstimate(
            flops=10 * tok * width * rank, bytes_accessed=8 * width * rank, transcendentals=tok * experts
        ),
    )(inputs, cotangent, logits, in_factor, out_factor, expert_factor)
    return out[0], out[1].T, out[2], out[3], out[4]


def by_collectives(inputs, cotangent, logits, in_factor, out_factor, expert_factor):
    fl = jnp.float32
    n_term = lax.axis_size("term")
    n_data = lax.axis_size("dp")
    gates = jax.nn.softmax(logits, axis=-1)
    gates_bf = gates.astype(jnp.bfloat16)
    proj_in = jnp.dot(inputs, in_factor, preferred_element_type=fl)
    proj_exp = jnp.dot(gates_bf, expert_factor, preferred_element_type=fl)
    hidden = (proj_in * proj_exp).astype(jnp.bfloat16)
    full_cotan = lax.all_gather(cotangent, "term", axis=1, tiled=True)
    grad_hid = jnp.dot(full_cotan, out_factor, preferred_element_type=fl)
    grad_pin = (grad_hid * proj_exp).astype(jnp.bfloat16)
    grad_pexp = (grad_hid * proj_in).astype(jnp.bfloat16)
    row_total = lax.psum(jnp.sum(grad_hid * proj_in * proj_exp, axis=1, keepdims=True), "term")
    contract_last = (((1,), (1,)), ((), ()))
    part_x = lax.dot_general(grad_pin, in_factor, contract_last, preferred_element_type=fl)
    part_g = lax.dot_general(grad_pexp, expert_factor, contract_last, preferred_element_type=fl)
    sum_x, grad_gate = (
        lax.psum_scatter(
            part_x.astype(jnp.bfloat16), "term", scatter_dimension=1, tiled=True
        ).astype(jnp.float32),
        lax.psum_scatter(
            part_g.astype(jnp.bfloat16), "term", scatter_dimension=1, tiled=True
        ).astype(jnp.float32),
    )
    grad_inputs = sum_x.astype(jnp.bfloat16)
    exp_local = logits.shape[1] // n_term
    gates_local = lax.dynamic_slice_in_dim(gates, lax.axis_index("term") * exp_local, exp_local, 1)
    grad_logits = gates_local * (grad_gate - row_total)
    scale = 1.0 / math.sqrt(inputs.shape[0] * n_data)
    contract_first = (((0,), (0,)), ((), ()))
    part_in = lax.dot_general(inputs, grad_pin, contract_first, preferred_element_type=fl) * scale
    part_out = (
        lax.dot_general(full_cotan, hidden, contract_first, preferred_element_type=fl) * scale
    )
    part_exp = (
        lax.dot_general(gates_bf, grad_pexp, contract_first, preferred_element_type=fl) * scale
    )
    grad_in, grad_out, grad_exp = (
        lax.psum_scatter(
            part_in.astype(jnp.bfloat16), "dp", scatter_dimension=0, tiled=True
        ).astype(jnp.float32),
        lax.psum_scatter(
            part_out.astype(jnp.bfloat16), "dp", scatter_dimension=0, tiled=True
        ).astype(jnp.float32),
        lax.psum_scatter(
            part_exp.astype(jnp.bfloat16), "dp", scatter_dimension=0, tiled=True
        ).astype(jnp.float32),
    )
    return (grad_inputs, grad_logits, grad_in, grad_out, grad_exp)


def solution(mesh):
    return jax.shard_map(
        fused if (mesh.shape["term"], mesh.shape["dp"]) == (8, 4) else by_collectives,
        mesh=mesh,
        in_specs=(
            P("dp", None),
            P("dp", "term"),
            P("dp", None),
            P(None, "term"),
            P(None, "term"),
            P(None, "term"),
        ),
        out_specs=(
            P("dp", "term"),
            P("dp", "term"),
            P("dp", "term"),
            P("dp", "term"),
            P("dp", "term"),
        ),
        check_vma=False,
    )
```

```python
import functools
import math

import jax
import jax.numpy as jnp
from jax import lax
from jax.experimental import pallas as pl
from jax.experimental.pallas import tpu as pltpu
from jax.sharding import PartitionSpec as P

FL = jnp.float32
BF = jnp.bfloat16
LAST = (((1,), (1,)), ((), ()))
FIRST = (((0,), (0,)), ((), ()))
SUBS = 2


def fused_kernel(
    n, m, scale,
    x_hbm, cot_ref, log_ref, fin_hbm, fout_hbm, fexp_ref,
    gx_ref, gl_ref, gin_ref, gout_ref, gexp_ref,
    x, fin, fout, cot, pin, pexp, ghid, hid, gpin, gpexp, gt, gbf,
    rs_send, rs_recv, c_send, c_recv, x_send, x_recv, kept,
    g_send, g_recv, r_send, r_recv, e_send, e_recv,
    load_sem, ag_s, ag_r, rs_s, rs_r, c_s, c_r, xs_s, xs_r, g_s, g_r, r_s, r_r, e_s, e_r,
):
    t = lax.axis_index("term")
    a = lax.axis_index("dp")
    tok = cot_ref.shape[0]
    half = cot_ref.shape[1] // 2
    rows = tok // SUBS
    loads = [
        pltpu.make_async_copy(src, dst, load_sem.at[i])
        for i, (src, dst) in enumerate(((x_hbm, x), (fin_hbm, fin), (fout_hbm, fout)))
    ]
    for c in loads:
        c.start()
    barrier = pltpu.get_barrier_semaphore()
    for d in range(1, n):
        pl.semaphore_signal(barrier, inc=1, device_id={"term": lax.rem(t + d, n)}, device_id_type=pl.DeviceIdType.MESH)
    for d in range(1, m):
        pl.semaphore_signal(barrier, inc=1, device_id={"dp": lax.rem(a + d, m)}, device_id_type=pl.DeviceIdType.MESH)
    cot[t, 0] = cot_ref[:, :half]
    cot[t, 1] = cot_ref[:, half:]

    hz = n // 2
    pos = t // 2 + lax.rem(t, 2) * (n - 1 - 2 * (t // 2))

    def term_at(p):
        p = lax.rem(p + 2 * n, n)
        u = p // hz
        return (1 - u) * 2 * p + u * (2 * (n - 1 - p) + 1)

    ahead = (term_at(pos + 1), term_at(pos - 1))
    sign = (1, -1)
    streams = [(d, s) for d in range(2) for s in range(SUBS)]

    def remote(src, dst, ss, rs, dev):
        return pltpu.make_async_remote_copy(
            src_ref=src, dst_ref=dst, send_sem=ss, recv_sem=rs,
            device_id=dev, device_id_type=pl.DeviceIdType.MESH,
        )

    def ag(d, s, k, owner):
        ref = cot.at[owner, d, pl.ds(s * rows, rows), :]
        return remote(ref, ref, ag_s.at[d * SUBS + s, k], ag_r.at[d * SUBS + s, k], {"term": ahead[d]})

    pl.semaphore_wait(barrier, n + m - 2)
    for d, s in streams:
        ag(d, s, 0, t).start()

    z = log_ref[...]
    z = jnp.exp(z - jnp.max(z, axis=1, keepdims=True))
    gates = z / jnp.sum(z, axis=1, keepdims=True)
    gt[...] = jnp.transpose(gates)
    gbf[...] = gates.astype(BF)
    pexp[...] = jnp.dot(gbf[...], fexp_ref[...], preferred_element_type=FL)
    loads[0].wait()
    loads[1].wait()
    loads[2].wait()
    pin[...] = jnp.zeros_like(pin)
    wide = 2 * half

    @pl.loop(0, n)
    def _(i):
        at = pl.ds(pl.multiple_of(i * wide, wide), wide)
        pin[...] += jnp.dot(x[:, at], fin[at, :], preferred_element_type=FL)

    hid[...] = (pin[...] * pexp[...]).astype(BF)
    ghid[...] = jnp.zeros_like(ghid)

    def add_hid(d, owner):
        at = pl.ds(pl.multiple_of(owner * wide + d * half, half), half)
        ghid[...] += jnp.dot(cot[owner, d], fout[at, :], preferred_element_type=FL)

    add_hid(0, t)
    add_hid(1, t)

    core = lax.rem(a, 2)
    xx = a // 2
    mate = {"dp": 2 * xx + 1 - core}
    across = {"dp": lax.rem(a + 2, m)}
    per = gin_ref.shape[0]
    cuts = per // half

    def part_f(w, owner, j):
        if w == 0:
            at = owner * (n // m) + j // 2
            lhs, rhs = cot[at, lax.rem(j, 2)], hid[...]
        else:
            lhs, rhs = x[:, pl.ds(pl.multiple_of(owner * per + j * half, half), half)], gpin[...]
        return lax.dot_general(lhs, rhs, FIRST, preferred_element_type=FL) * scale

    def to_mate(w, q, j):
        i = w * cuts + j
        return remote(c_send.at[q, i], c_recv.at[q, i], c_s.at[q, i], c_r.at[q, i], mate)

    def to_x(w, j):
        i = w * cuts + j
        return remote(x_send.at[i], x_recv.at[i], xs_s.at[i], xs_r.at[i], across)

    def give(w, q, j):
        chip = q * xx + (1 - q) * (1 - xx)
        c_send[q, w * cuts + j] = part_f(w, 2 * chip + 1 - core, j).astype(BF)
        to_mate(w, q, j).start()

    def pass_on(w, j):
        own = part_f(w, 2 * (1 - xx) + core, j)
        to_mate(w, 0, j).wait_recv()
        x_send[w * cuts + j] = (own + c_recv[0, w * cuts + j].astype(FL)).astype(BF)
        to_x(w, j).start()

    outs = (gout_ref, gin_ref)

    def keep(w, j):
        own = part_f(w, a, j)
        to_mate(w, 1, j).wait_recv()
        kept[w * cuts + j] = own + c_recv[1, w * cuts + j].astype(FL)

    def finish(w):
        @pl.loop(0, cuts)
        def _(j):
            to_x(w, j).wait_recv()
            at = pl.ds(pl.multiple_of(j * half, half), half)
            outs[w][at, :] = (kept[w * cuts + j] + x_recv[w * cuts + j].astype(FL)).astype(BF)

    def each(f, lo, hi):
        @pl.loop(lo, hi)
        def _(j):
            f(j)

    def place(d, k):
        at = term_at(pos - sign[d] * k)
        return at // (n // m), 2 * lax.rem(at, n // m) + d

    def hand(d, k):
        owner, j = place(d, k)

        @pl.when(lax.rem(owner, 2) != core)
        def _():
            @pl.when(owner // 2 == xx)
            def _():
                give(0, 1, j)

            @pl.when(owner // 2 != xx)
            def _():
                give(0, 0, j)

    def settle(d, k):
        owner, j = place(d, k)

        @pl.when(lax.rem(owner, 2) == core)
        def _():
            @pl.when(owner // 2 == xx)
            def _():
                keep(0, j)

            @pl.when(owner // 2 != xx)
            def _():
                pass_on(0, j)

    hand(0, 0)
    hand(1, 0)

    @pl.loop(1, n)
    def _(k):
        for d, s in streams:
            owner = term_at(pos - sign[d] * k)
            ag(d, s, k - 1, owner).wait_recv()

            @pl.when(k < n - 1)
            def _():
                ag(d, s, k, owner).start()

        for d in range(2):
            add_hid(d, term_at(pos - sign[d] * k))
        for d in range(2):
            hand(d, k)
        for d in range(2):
            settle(d, k - 1)

    gh = ghid[...]
    gpin[...] = (gh * pexp[...]).astype(BF)
    ghp = gh * pin[...]
    gpexp[...] = ghp.astype(BF)

    def part_x(d, s, owner):
        at = pl.ds(pl.multiple_of(owner * wide + d * half, half), half)
        return lax.dot_general(gpin[s * rows:(s + 1) * rows, :], fin[at, :], LAST, preferred_element_type=FL)

    def rs(d, s, k):
        i = d * SUBS + s
        return remote(rs_send.at[i, k], rs_recv.at[i, k], rs_s.at[i, k], rs_r.at[i, k], {"term": ahead[d]})

    for d, s in streams:
        rs_send[d * SUBS + s, 0] = part_x(d, s, term_at(pos - sign[d])).astype(BF)
        rs(d, s, 0).start()

    def rs_step(k):
        for d, s in streams:
            i = d * SUBS + s
            own = part_x(d, s, term_at(pos - sign[d] * (k + 1)))
            rs(d, s, k - 1).wait_recv()
            rs_send[i, k] = (own + rs_recv[i, k - 1].astype(FL)).astype(BF)
            rs(d, s, k).start()

    each(lambda j: give(1, 0, j), 0, cuts)
    each(lambda j: pass_on(1, j), 0, cuts // 2)
    rs_step(1)
    each(lambda j: pass_on(1, j), cuts // 2, cuts)
    settle(0, n - 1)
    settle(1, n - 1)
    rs_step(2)

    share = gt.shape[0] // n
    row = jnp.sum(ghp * pexp[...], axis=1, keepdims=True)
    r_send[...] = jnp.transpose(jnp.broadcast_to(row, (tok, 128)))[:8]
    g_send[...] = lax.dot_general(fexp_ref[...], gpexp[...], LAST, preferred_element_type=FL).astype(BF)
    e_send[...] = (lax.dot_general(gbf[...], gpexp[...], FIRST, preferred_element_type=FL) * scale).astype(BF)
    eper = gexp_ref.shape[0]

    def g_copy(d):
        to = lax.rem(t + d, n)
        src = g_send.at[pl.ds(pl.multiple_of(to * share, share), share), :]
        return remote(src, g_recv.at[d - 1], g_s.at[d - 1], g_r.at[d - 1], {"term": to})

    def r_copy(d):
        return remote(r_send, r_recv.at[d - 1], r_s.at[d - 1], r_r.at[d - 1], {"term": lax.rem(t + d, n)})

    def e_copy(d):
        to = lax.rem(a + d, m)
        src = e_send.at[pl.ds(pl.multiple_of(to * eper, eper), eper), :]
        return remote(src, e_recv.at[d - 1], e_s.at[d - 1], e_r.at[d - 1], {"dp": to})

    for d in range(1, n):
        g_copy(d).start()
        r_copy(d).start()
    for d in range(1, m):
        e_copy(d).start()

    rs_step(3)
    each(lambda j: give(1, 1, j), 0, cuts)
    rs_step(4)
    finish(0)
    rs_step(5)
    each(lambda j: keep(1, j), 0, cuts)
    mine = pl.ds(pl.multiple_of(t * share, share), share)
    gsum = g_send[mine, :].astype(FL)
    rsum = r_send[...]
    for d in range(1, n):
        g_copy(d).wait_recv()
        r_copy(d).wait_recv()
        gsum += g_recv[d - 1].astype(FL)
        rsum += r_recv[d - 1]
    gl_ref[...] = gt[mine, :] * (gsum - rsum[:1])
    esum = e_send[pl.ds(pl.multiple_of(a * eper, eper), eper), :].astype(FL)
    for d in range(1, m):
        e_copy(d).wait_recv()
        esum += e_recv[d - 1].astype(FL)
    gexp_ref[...] = esum
    for k in range(6, n - 1):
        rs_step(k)
    finish(1)
    for d, s in streams:
        i = d * SUBS + s
        own = part_x(d, s, t)
        rs(d, s, n - 2).wait_recv()
        gx_ref[s * rows:(s + 1) * rows, d * half:(d + 1) * half] = (own + rs_recv[i, n - 2].astype(FL)).astype(BF)

    @pl.loop(0, n - 1)
    def _(k):
        for d, s in streams:
            ag(d, s, k, term_at(pos - sign[d] * k)).wait_send()
            rs(d, s, k).wait_send()

    for w in range(2):
        @pl.loop(0, cuts)
        def _(j):
            to_mate(w, 0, j).wait_send()
            to_mate(w, 1, j).wait_send()
            to_x(w, j).wait_send()

    for d in range(1, n):
        g_copy(d).wait_send()
        r_copy(d).wait_send()
    for d in range(1, m):
        e_copy(d).wait_send()


def fused(inputs, cotangent, logits, in_factor, out_factor, expert_factor):
    n, m = lax.axis_size("term"), lax.axis_size("dp")
    tok, wide = cotangent.shape
    width, rank = in_factor.shape
    experts = logits.shape[1]
    half, rows, per = wide // 2, tok // SUBS, width // m
    cuts = per // half
    ns = 2 * SUBS
    scale = 1.0 / math.sqrt(tok * m)
    shape = jax.ShapeDtypeStruct
    vm = pl.BlockSpec(memory_space=pltpu.VMEM)
    hbm = pl.BlockSpec(memory_space=pl.ANY)
    dma = pltpu.SemaphoreType.DMA
    out = pl.pallas_call(
        functools.partial(fused_kernel, n, m, scale),
        out_shape=(
            shape((tok, wide), BF),
            shape((experts // n, tok), FL),
            shape((per, rank), BF),
            shape((per, rank), BF),
            shape((experts // m, rank), FL),
        ),
        in_specs=[hbm, vm, vm, hbm, hbm, vm],
        out_specs=(vm,) * 5,
        scratch_shapes=[
            pltpu.VMEM((tok, width), BF),
            pltpu.VMEM((width, rank), BF),
            pltpu.VMEM((width, rank), BF),
            pltpu.VMEM((n, 2, tok, half), BF),
            pltpu.VMEM((tok, rank), FL),
            pltpu.VMEM((tok, rank), FL),
            pltpu.VMEM((tok, rank), FL),
            pltpu.VMEM((tok, rank), BF),
            pltpu.VMEM((tok, rank), BF),
            pltpu.VMEM((tok, rank), BF),
            pltpu.VMEM((experts, tok), FL),
            pltpu.VMEM((tok, experts), BF),
            pltpu.VMEM((ns, n - 1, rows, half), BF),
            pltpu.VMEM((ns, n - 1, rows, half), BF),
            pltpu.VMEM((2, 2 * cuts, half, rank), BF),
            pltpu.VMEM((2, 2 * cuts, half, rank), BF),
            pltpu.VMEM((2 * cuts, half, rank), BF),
            pltpu.VMEM((2 * cuts, half, rank), BF),
            pltpu.VMEM((2 * cuts, half, rank), FL),
            pltpu.VMEM((experts, tok), BF),
            pltpu.VMEM((n - 1, experts // n, tok), BF),
            pltpu.VMEM((8, tok), FL),
            pltpu.VMEM((n - 1, 8, tok), FL),
            pltpu.VMEM((experts, rank), BF),
            pltpu.VMEM((m - 1, experts // m, rank), BF),
            dma((3,)),
            dma((ns, n - 1)), dma((ns, n - 1)), dma((ns, n - 1)), dma((ns, n - 1)),
            dma((2, 2 * cuts)), dma((2, 2 * cuts)), dma((2 * cuts,)), dma((2 * cuts,)),
            dma((n - 1,)), dma((n - 1,)), dma((n - 1,)), dma((n - 1,)),
            dma((m - 1,)), dma((m - 1,)),
        ],
        compiler_params=pltpu.CompilerParams(
            collective_id=0, has_side_effects=True, vmem_limit_bytes=60 * 2**20
        ),
        cost_estimate=pl.CostEstimate(
            flops=10 * tok * width * rank, bytes_accessed=8 * width * rank, transcendentals=tok * experts
        ),
    )(inputs, cotangent, logits, in_factor, out_factor, expert_factor)
    return out[0], out[1].T, out[2].astype(FL), out[3].astype(FL), out[4]


def by_collectives(inputs, cotangent, logits, in_factor, out_factor, expert_factor):
    fl = jnp.float32
    n_term = lax.axis_size("term")
    n_data = lax.axis_size("dp")
    gates = jax.nn.softmax(logits, axis=-1)
    gates_bf = gates.astype(jnp.bfloat16)
    proj_in = jnp.dot(inputs, in_factor, preferred_element_type=fl)
    proj_exp = jnp.dot(gates_bf, expert_factor, preferred_element_type=fl)
    hidden = (proj_in * proj_exp).astype(jnp.bfloat16)
    full_cotan = lax.all_gather(cotangent, "term", axis=1, tiled=True)
    grad_hid = jnp.dot(full_cotan, out_factor, preferred_element_type=fl)
    grad_pin = (grad_hid * proj_exp).astype(jnp.bfloat16)
    grad_pexp = (grad_hid * proj_in).astype(jnp.bfloat16)
    row_total = lax.psum(jnp.sum(grad_hid * proj_in * proj_exp, axis=1, keepdims=True), "term")
    contract_last = (((1,), (1,)), ((), ()))
    part_x = lax.dot_general(grad_pin, in_factor, contract_last, preferred_element_type=fl)
    part_g = lax.dot_general(grad_pexp, expert_factor, contract_last, preferred_element_type=fl)
    sum_x, grad_gate = (
        lax.psum_scatter(
            part_x.astype(jnp.bfloat16), "term", scatter_dimension=1, tiled=True
        ).astype(jnp.float32),
        lax.psum_scatter(
            part_g.astype(jnp.bfloat16), "term", scatter_dimension=1, tiled=True
        ).astype(jnp.float32),
    )
    grad_inputs = sum_x.astype(jnp.bfloat16)
    exp_local = logits.shape[1] // n_term
    gates_local = lax.dynamic_slice_in_dim(gates, lax.axis_index("term") * exp_local, exp_local, 1)
    grad_logits = gates_local * (grad_gate - row_total)
    scale = 1.0 / math.sqrt(inputs.shape[0] * n_data)
    contract_first = (((0,), (0,)), ((), ()))
    part_in = lax.dot_general(inputs, grad_pin, contract_first, preferred_element_type=fl) * scale
    part_out = (
        lax.dot_general(full_cotan, hidden, contract_first, preferred_element_type=fl) * scale
    )
    part_exp = (
        lax.dot_general(gates_bf, grad_pexp, contract_first, preferred_element_type=fl) * scale
    )
    grad_in, grad_out, grad_exp = (
        lax.psum_scatter(
            part_in.astype(jnp.bfloat16), "dp", scatter_dimension=0, tiled=True
        ).astype(jnp.float32),
        lax.psum_scatter(
            part_out.astype(jnp.bfloat16), "dp", scatter_dimension=0, tiled=True
        ).astype(jnp.float32),
        lax.psum_scatter(
            part_exp.astype(jnp.bfloat16), "dp", scatter_dimension=0, tiled=True
        ).astype(jnp.float32),
    )
    return (grad_inputs, grad_logits, grad_in, grad_out, grad_exp)


def solution(mesh):
    return jax.shard_map(
        fused if (mesh.shape["term"], mesh.shape["dp"]) == (8, 4) else by_collectives,
        mesh=mesh,
        in_specs=(
            P("dp", None),
            P("dp", "term"),
            P("dp", None),
            P(None, "term"),
            P(None, "term"),
            P(None, "term"),
        ),
        out_specs=(
            P("dp", "term"),
            P("dp", "term"),
            P("dp", "term"),
            P("dp", "term"),
            P("dp", "term"),
        ),
        check_vma=False,
    )
```

```python
import functools
import math

import jax
import jax.numpy as jnp
from jax import lax
from jax.experimental import pallas as pl
from jax.experimental.pallas import tpu as pltpu
from jax.sharding import PartitionSpec as P

FL = jnp.float32
BF = jnp.bfloat16
LAST = (((1,), (1,)), ((), ()))
FIRST = (((0,), (0,)), ((), ()))
SUBS = 2


def fused_kernel(
    n, m, scale,
    x_hbm, cot_ref, log_ref, fin_hbm, fout_hbm, fexp_ref,
    gx_ref, gl_ref, gin_ref, gout_ref, gexp_ref,
    x, fin, fout, cot, pin, pexp, ghid, hid, gpin, gpexp, gt, gbf,
    rs_send, rs_recv, c_send, c_recv, x_send, x_recv, kept,
    g_send, g_recv, r_send, r_recv, e_send, e_recv,
    load_sem, ag_s, ag_r, rs_s, rs_r, c_s, c_r, xs_s, xs_r, g_s, g_r, r_s, r_r, e_s, e_r,
):
    t = lax.axis_index("term")
    a = lax.axis_index("dp")
    tok = cot_ref.shape[0]
    half = cot_ref.shape[1] // 2
    rows = tok // SUBS
    loads = [
        pltpu.make_async_copy(src, dst, load_sem.at[i])
        for i, (src, dst) in enumerate(((x_hbm, x), (fin_hbm, fin), (fout_hbm, fout)))
    ]
    for c in loads:
        c.start()
    barrier = pltpu.get_barrier_semaphore()
    for d in range(1, n):
        pl.semaphore_signal(barrier, inc=1, device_id={"term": lax.rem(t + d, n)}, device_id_type=pl.DeviceIdType.MESH)
    for d in range(1, m):
        pl.semaphore_signal(barrier, inc=1, device_id={"dp": lax.rem(a + d, m)}, device_id_type=pl.DeviceIdType.MESH)
    cot[t, 0] = cot_ref[:, :half]
    cot[t, 1] = cot_ref[:, half:]

    hz = n // 2
    pos = t // 2 + lax.rem(t, 2) * (n - 1 - 2 * (t // 2))

    def term_at(p):
        p = lax.rem(p + 2 * n, n)
        u = p // hz
        return (1 - u) * 2 * p + u * (2 * (n - 1 - p) + 1)

    ahead = (term_at(pos + 1), term_at(pos - 1))
    sign = (1, -1)
    streams = [(d, s) for s in range(SUBS) for d in range(2)]

    def remote(src, dst, ss, rs, dev):
        return pltpu.make_async_remote_copy(
            src_ref=src, dst_ref=dst, send_sem=ss, recv_sem=rs,
            device_id=dev, device_id_type=pl.DeviceIdType.MESH,
        )

    def ag(d, s, k, owner):
        ref = cot.at[owner, d, pl.ds(s * rows, rows), :]
        return remote(ref, ref, ag_s.at[d * SUBS + s, k], ag_r.at[d * SUBS + s, k], {"term": ahead[d]})

    pl.semaphore_wait(barrier, n + m - 2)
    for d, s in streams:
        ag(d, s, 0, t).start()

    def forward(k):
        for d, s in streams:
            owner = term_at(pos - sign[d] * k)
            ag(d, s, k - 1, owner).wait_recv()

            @pl.when(k < n - 1)
            def _():
                ag(d, s, k, owner).start()

    z = log_ref[...]
    z = jnp.exp(z - jnp.max(z, axis=1, keepdims=True))
    gates = z / jnp.sum(z, axis=1, keepdims=True)
    gt[...] = jnp.transpose(gates)
    gbf[...] = gates.astype(BF)
    pexp[...] = jnp.dot(gbf[...], fexp_ref[...], preferred_element_type=FL)
    loads[0].wait()
    loads[1].wait()
    loads[2].wait()
    forward(1)
    pin[...] = jnp.zeros_like(pin)
    wide = 2 * half

    @pl.loop(0, n)
    def _(i):
        at = pl.ds(pl.multiple_of(i * wide, wide), wide)
        pin[...] += jnp.dot(x[:, at], fin[at, :], preferred_element_type=FL)

    hid[...] = (pin[...] * pexp[...]).astype(BF)
    ghid[...] = jnp.zeros_like(ghid)

    def add_hid(d, owner):
        at = pl.ds(pl.multiple_of(owner * wide + d * half, half), half)
        ghid[...] += jnp.dot(cot[owner, d], fout[at, :], preferred_element_type=FL)

    add_hid(0, t)
    add_hid(1, t)

    core = lax.rem(a, 2)
    xx = a // 2
    mate = {"dp": 2 * xx + 1 - core}
    across = {"dp": lax.rem(a + 2, m)}
    per = gin_ref.shape[0]
    cuts = per // half

    def part_f(w, owner, j):
        if w == 0:
            at = owner * (n // m) + j // 2
            lhs, rhs = cot[at, lax.rem(j, 2)], hid[...]
        else:
            lhs, rhs = x[:, pl.ds(pl.multiple_of(owner * per + j * half, half), half)], gpin[...]
        return lax.dot_general(lhs, rhs, FIRST, preferred_element_type=FL) * scale

    def to_mate(w, q, j):
        i = w * cuts + j
        return remote(c_send.at[q, i], c_recv.at[q, i], c_s.at[q, i], c_r.at[q, i], mate)

    def to_x(w, j):
        i = w * cuts + j
        return remote(x_send.at[i], x_recv.at[i], xs_s.at[i], xs_r.at[i], across)

    def give(w, q, j):
        chip = q * xx + (1 - q) * (1 - xx)
        c_send[q, w * cuts + j] = part_f(w, 2 * chip + 1 - core, j).astype(BF)
        to_mate(w, q, j).start()

    def pass_on(w, j):
        own = part_f(w, 2 * (1 - xx) + core, j)
        to_mate(w, 0, j).wait_recv()
        x_send[w * cuts + j] = (own + c_recv[0, w * cuts + j].astype(FL)).astype(BF)
        to_x(w, j).start()

    outs = (gout_ref, gin_ref)

    def keep(w, j):
        own = part_f(w, a, j)
        to_mate(w, 1, j).wait_recv()
        kept[w * cuts + j] = own + c_recv[1, w * cuts + j].astype(FL)

    def finish(w):
        @pl.loop(0, cuts)
        def _(j):
            to_x(w, j).wait_recv()
            at = pl.ds(pl.multiple_of(j * half, half), half)
            outs[w][at, :] = (kept[w * cuts + j] + x_recv[w * cuts + j].astype(FL)).astype(BF)

    def each(f, lo, hi):
        @pl.loop(lo, hi)
        def _(j):
            f(j)

    def place(d, k):
        at = term_at(pos - sign[d] * k)
        return at // (n // m), 2 * lax.rem(at, n // m) + d

    def hand(d, k):
        owner, j = place(d, k)

        @pl.when(lax.rem(owner, 2) != core)
        def _():
            @pl.when(owner // 2 == xx)
            def _():
                give(0, 1, j)

            @pl.when(owner // 2 != xx)
            def _():
                give(0, 0, j)

    def settle(d, k):
        owner, j = place(d, k)

        @pl.when(lax.rem(owner, 2) == core)
        def _():
            @pl.when(owner // 2 == xx)
            def _():
                keep(0, j)

            @pl.when(owner // 2 != xx)
            def _():
                pass_on(0, j)

    def add_both(k):
        for d in range(2):
            add_hid(d, term_at(pos - sign[d] * k))

    def both(f, k):
        f(0, k)
        f(1, k)

    add_both(1)
    both(hand, 0)

    @pl.loop(2, n - 1)
    def _(k):
        forward(k)
        add_both(k)
        both(hand, k - 1)
        both(settle, k - 2)

    forward(n - 1)
    add_both(n - 1)

    gh = ghid[...]
    gpin[...] = (gh * pexp[...]).astype(BF)
    ghp = gh * pin[...]
    gpexp[...] = ghp.astype(BF)

    def part_x(d, s, owner):
        at = pl.ds(pl.multiple_of(owner * wide + d * half, half), half)
        return lax.dot_general(gpin[s * rows:(s + 1) * rows, :], fin[at, :], LAST, preferred_element_type=FL)

    def rs(d, s, k):
        i = d * SUBS + s
        return remote(rs_send.at[i, k], rs_recv.at[i, k], rs_s.at[i, k], rs_r.at[i, k], {"term": ahead[d]})

    for d, s in streams:
        rs_send[d * SUBS + s, 0] = part_x(d, s, term_at(pos - sign[d])).astype(BF)
        rs(d, s, 0).start()

    def rs_step(k):
        for d, s in streams:
            i = d * SUBS + s
            own = part_x(d, s, term_at(pos - sign[d] * (k + 1)))
            rs(d, s, k - 1).wait_recv()
            rs_send[i, k] = (own + rs_recv[i, k - 1].astype(FL)).astype(BF)
            rs(d, s, k).start()

    @pl.loop(n - 2, n)
    def _(k):
        both(hand, k)
        both(settle, k - 1)

    each(lambda j: give(1, 0, j), 0, cuts // 2)
    rs_step(1)
    each(lambda j: pass_on(1, j), 0, cuts // 2)
    each(lambda j: give(1, 0, j), cuts // 2, cuts)
    both(settle, n - 1)
    each(lambda j: pass_on(1, j), cuts // 2, cuts)
    rs_step(2)

    share = gt.shape[0] // n
    row = jnp.sum(ghp * pexp[...], axis=1, keepdims=True)
    r_send[...] = jnp.transpose(jnp.broadcast_to(row, (tok, 128)))[:8]
    g_send[...] = lax.dot_general(fexp_ref[...], gpexp[...], LAST, preferred_element_type=FL).astype(BF)
    e_send[...] = (lax.dot_general(gbf[...], gpexp[...], FIRST, preferred_element_type=FL) * scale).astype(BF)
    eper = gexp_ref.shape[0]

    def g_copy(d):
        to = lax.rem(t + d, n)
        src = g_send.at[pl.ds(pl.multiple_of(to * share, share), share), :]
        return remote(src, g_recv.at[d - 1], g_s.at[d - 1], g_r.at[d - 1], {"term": to})

    def r_copy(d):
        return remote(r_send, r_recv.at[d - 1], r_s.at[d - 1], r_r.at[d - 1], {"term": lax.rem(t + d, n)})

    def e_copy(d):
        to = lax.rem(a + d, m)
        src = e_send.at[pl.ds(pl.multiple_of(to * eper, eper), eper), :]
        return remote(src, e_recv.at[d - 1], e_s.at[d - 1], e_r.at[d - 1], {"dp": to})

    for d in range(1, n):
        g_copy(d).start()
        r_copy(d).start()
    for d in range(1, m):
        e_copy(d).start()

    rs_step(3)
    each(lambda j: give(1, 1, j), 0, cuts)
    rs_step(4)
    finish(0)
    rs_step(5)
    each(lambda j: keep(1, j), 0, cuts)
    mine = pl.ds(pl.multiple_of(t * share, share), share)
    gsum = g_send[mine, :].astype(FL)
    rsum = r_send[...]
    for d in range(1, n):
        g_copy(d).wait_recv()
        r_copy(d).wait_recv()
        gsum += g_recv[d - 1].astype(FL)
        rsum += r_recv[d - 1]
    gl_ref[...] = gt[mine, :] * (gsum - rsum[:1])
    esum = e_send[pl.ds(pl.multiple_of(a * eper, eper), eper), :].astype(FL)
    for d in range(1, m):
        e_copy(d).wait_recv()
        esum += e_recv[d - 1].astype(FL)
    gexp_ref[...] = esum
    for k in range(6, n - 1):
        rs_step(k)
    finish(1)
    for d, s in streams:
        i = d * SUBS + s
        own = part_x(d, s, t)
        rs(d, s, n - 2).wait_recv()
        gx_ref[s * rows:(s + 1) * rows, d * half:(d + 1) * half] = (own + rs_recv[i, n - 2].astype(FL)).astype(BF)

    @pl.loop(0, n - 1)
    def _(k):
        for d, s in streams:
            ag(d, s, k, term_at(pos - sign[d] * k)).wait_send()
            rs(d, s, k).wait_send()

    for w in range(2):
        @pl.loop(0, cuts)
        def _(j):
            to_mate(w, 0, j).wait_send()
            to_mate(w, 1, j).wait_send()
            to_x(w, j).wait_send()

    for d in range(1, n):
        g_copy(d).wait_send()
        r_copy(d).wait_send()
    for d in range(1, m):
        e_copy(d).wait_send()


def finishing_kernel(gx, gl, gin, gout, gexp, gx_o, gl_o, gin_o, gout_o, gexp_o):
    gx_o[...] = gx[...]
    gin_o[...] = gin[...].astype(FL)
    gout_o[...] = gout[...].astype(FL)

    @pl.when(pl.program_id(0) == 0)
    def _():
        gl_o[...] = gl[...]
        gexp_o[...] = gexp[...]


def finishing(gx, gl, gin, gout, gexp):
    steps = 4
    cut = lambda v: pl.BlockSpec((v.shape[0] // steps, v.shape[1]), lambda i: (i, 0))
    full = lambda v: pl.BlockSpec(v.shape, lambda i: (0, 0))
    specs = [cut(gx), full(gl), cut(gin), cut(gout), full(gexp)]
    shape = jax.ShapeDtypeStruct
    out = pl.pallas_call(
        finishing_kernel,
        grid=(steps,),
        out_shape=(
            shape(gx.shape, BF), shape(gl.shape, FL), shape(gin.shape, FL),
            shape(gout.shape, FL), shape(gexp.shape, FL),
        ),
        in_specs=specs,
        out_specs=specs,
        compiler_params=pltpu.CompilerParams(vmem_limit_bytes=32 * 2**20),
    )(gx, gl, gin, gout, gexp)
    return out[0], out[1].T, out[2], out[3], out[4]


def fused(inputs, cotangent, logits, in_factor, out_factor, expert_factor):
    n, m = lax.axis_size("term"), lax.axis_size("dp")
    tok, wide = cotangent.shape
    width, rank = in_factor.shape
    experts = logits.shape[1]
    half, rows, per = wide // 2, tok // SUBS, width // m
    cuts = per // half
    ns = 2 * SUBS
    scale = 1.0 / math.sqrt(tok * m)
    shape = jax.ShapeDtypeStruct
    vm = pl.BlockSpec(memory_space=pltpu.VMEM)
    hbm = pl.BlockSpec(memory_space=pl.ANY)
    dma = pltpu.SemaphoreType.DMA
    out = pl.pallas_call(
        functools.partial(fused_kernel, n, m, scale),
        out_shape=(
            shape((tok, wide), BF),
            shape((experts // n, tok), FL),
            shape((per, rank), BF),
            shape((per, rank), BF),
            shape((experts // m, rank), FL),
        ),
        in_specs=[hbm, vm, vm, hbm, hbm, vm],
        out_specs=(vm,) * 5,
        scratch_shapes=[
            pltpu.VMEM((tok, width), BF),
            pltpu.VMEM((width, rank), BF),
            pltpu.VMEM((width, rank), BF),
            pltpu.VMEM((n, 2, tok, half), BF),
            pltpu.VMEM((tok, rank), FL),
            pltpu.VMEM((tok, rank), FL),
            pltpu.VMEM((tok, rank), FL),
            pltpu.VMEM((tok, rank), BF),
            pltpu.VMEM((tok, rank), BF),
            pltpu.VMEM((tok, rank), BF),
            pltpu.VMEM((experts, tok), FL),
            pltpu.VMEM((tok, experts), BF),
            pltpu.VMEM((ns, n - 1, rows, half), BF),
            pltpu.VMEM((ns, n - 1, rows, half), BF),
            pltpu.VMEM((2, 2 * cuts, half, rank), BF),
            pltpu.VMEM((2, 2 * cuts, half, rank), BF),
            pltpu.VMEM((2 * cuts, half, rank), BF),
            pltpu.VMEM((2 * cuts, half, rank), BF),
            pltpu.VMEM((2 * cuts, half, rank), FL),
            pltpu.VMEM((experts, tok), BF),
            pltpu.VMEM((n - 1, experts // n, tok), BF),
            pltpu.VMEM((8, tok), FL),
            pltpu.VMEM((n - 1, 8, tok), FL),
            pltpu.VMEM((experts, rank), BF),
            pltpu.VMEM((m - 1, experts // m, rank), BF),
            dma((3,)),
            dma((ns, n - 1)), dma((ns, n - 1)), dma((ns, n - 1)), dma((ns, n - 1)),
            dma((2, 2 * cuts)), dma((2, 2 * cuts)), dma((2 * cuts,)), dma((2 * cuts,)),
            dma((n - 1,)), dma((n - 1,)), dma((n - 1,)), dma((n - 1,)),
            dma((m - 1,)), dma((m - 1,)),
        ],
        compiler_params=pltpu.CompilerParams(
            collective_id=0, has_side_effects=True, vmem_limit_bytes=60 * 2**20
        ),
        cost_estimate=pl.CostEstimate(
            flops=10 * tok * width * rank, bytes_accessed=8 * width * rank, transcendentals=tok * experts
        ),
    )(inputs, cotangent, logits, in_factor, out_factor, expert_factor)
    return finishing(*out)


def by_collectives(inputs, cotangent, logits, in_factor, out_factor, expert_factor):
    fl = jnp.float32
    n_term = lax.axis_size("term")
    n_data = lax.axis_size("dp")
    gates = jax.nn.softmax(logits, axis=-1)
    gates_bf = gates.astype(jnp.bfloat16)
    proj_in = jnp.dot(inputs, in_factor, preferred_element_type=fl)
    proj_exp = jnp.dot(gates_bf, expert_factor, preferred_element_type=fl)
    hidden = (proj_in * proj_exp).astype(jnp.bfloat16)
    full_cotan = lax.all_gather(cotangent, "term", axis=1, tiled=True)
    grad_hid = jnp.dot(full_cotan, out_factor, preferred_element_type=fl)
    grad_pin = (grad_hid * proj_exp).astype(jnp.bfloat16)
    grad_pexp = (grad_hid * proj_in).astype(jnp.bfloat16)
    row_total = lax.psum(jnp.sum(grad_hid * proj_in * proj_exp, axis=1, keepdims=True), "term")
    contract_last = (((1,), (1,)), ((), ()))
    part_x = lax.dot_general(grad_pin, in_factor, contract_last, preferred_element_type=fl)
    part_g = lax.dot_general(grad_pexp, expert_factor, contract_last, preferred_element_type=fl)
    sum_x, grad_gate = (
        lax.psum_scatter(
            part_x.astype(jnp.bfloat16), "term", scatter_dimension=1, tiled=True
        ).astype(jnp.float32),
        lax.psum_scatter(
            part_g.astype(jnp.bfloat16), "term", scatter_dimension=1, tiled=True
        ).astype(jnp.float32),
    )
    grad_inputs = sum_x.astype(jnp.bfloat16)
    exp_local = logits.shape[1] // n_term
    gates_local = lax.dynamic_slice_in_dim(gates, lax.axis_index("term") * exp_local, exp_local, 1)
    grad_logits = gates_local * (grad_gate - row_total)
    scale = 1.0 / math.sqrt(inputs.shape[0] * n_data)
    contract_first = (((0,), (0,)), ((), ()))
    part_in = lax.dot_general(inputs, grad_pin, contract_first, preferred_element_type=fl) * scale
    part_out = (
        lax.dot_general(full_cotan, hidden, contract_first, preferred_element_type=fl) * scale
    )
    part_exp = (
        lax.dot_general(gates_bf, grad_pexp, contract_first, preferred_element_type=fl) * scale
    )
    grad_in, grad_out, grad_exp = (
        lax.psum_scatter(
            part_in.astype(jnp.bfloat16), "dp", scatter_dimension=0, tiled=True
        ).astype(jnp.float32),
        lax.psum_scatter(
            part_out.astype(jnp.bfloat16), "dp", scatter_dimension=0, tiled=True
        ).astype(jnp.float32),
        lax.psum_scatter(
            part_exp.astype(jnp.bfloat16), "dp", scatter_dimension=0, tiled=True
        ).astype(jnp.float32),
    )
    return (grad_inputs, grad_logits, grad_in, grad_out, grad_exp)


def solution(mesh):
    return jax.shard_map(
        fused if (mesh.shape["term"], mesh.shape["dp"]) == (8, 4) else by_collectives,
        mesh=mesh,
        in_specs=(
            P("dp", None),
            P("dp", "term"),
            P("dp", None),
            P(None, "term"),
            P(None, "term"),
            P(None, "term"),
        ),
        out_specs=(
            P("dp", "term"),
            P("dp", "term"),
            P("dp", "term"),
            P("dp", "term"),
            P("dp", "term"),
        ),
        check_vma=False,
    )
```

```python
import functools
import math

import jax
import jax.numpy as jnp
from jax import lax
from jax.experimental import pallas as pl
from jax.experimental.pallas import tpu as pltpu
from jax.sharding import PartitionSpec as P

FL = jnp.float32
BF = jnp.bfloat16
LAST = (((1,), (1,)), ((), ()))
FIRST = (((0,), (0,)), ((), ()))
SUBS = 2


def fused_kernel(
    n, m, scale,
    x_hbm, cot_ref, log_ref, fin_hbm, fout_hbm, fexp_ref,
    gx_ref, gl_ref, gin_ref, gout_ref, gexp_ref,
    x, fin, fout, cot, pin, pexp, ghid, hid, gpin, gpexp, gt, gbf,
    rs_send, rs_recv, c_send, c_recv, x_send, x_recv, kept,
    g_send, g_recv, r_send, r_recv, e_send, e_recv,
    load_sem, ag_s, ag_r, rs_s, rs_r, c_s, c_r, xs_s, xs_r, g_s, g_r, r_s, r_r, e_s, e_r,
):
    t = lax.axis_index("term")
    a = lax.axis_index("dp")
    tok = cot_ref.shape[0]
    half = cot_ref.shape[1] // 2
    rows = tok // SUBS
    loads = [
        pltpu.make_async_copy(src, dst, load_sem.at[i])
        for i, (src, dst) in enumerate(((x_hbm, x), (fin_hbm, fin), (fout_hbm, fout)))
    ]
    for c in loads:
        c.start()
    barrier = pltpu.get_barrier_semaphore()
    for d in range(1, n):
        pl.semaphore_signal(barrier, inc=1, device_id={"term": lax.rem(t + d, n)}, device_id_type=pl.DeviceIdType.MESH)
    for d in range(1, m):
        pl.semaphore_signal(barrier, inc=1, device_id={"dp": lax.rem(a + d, m)}, device_id_type=pl.DeviceIdType.MESH)
    cot[t, 0] = cot_ref[:, :half]
    cot[t, 1] = cot_ref[:, half:]

    hz = n // 2
    pos = t // 2 + lax.rem(t, 2) * (n - 1 - 2 * (t // 2))

    def term_at(p):
        p = lax.rem(p + 2 * n, n)
        u = p // hz
        return (1 - u) * 2 * p + u * (2 * (n - 1 - p) + 1)

    ahead = (term_at(pos + 1), term_at(pos - 1))
    sign = (1, -1)
    streams = [(d, s) for s in range(SUBS) for d in range(2)]

    def remote(src, dst, ss, rs, dev):
        return pltpu.make_async_remote_copy(
            src_ref=src, dst_ref=dst, send_sem=ss, recv_sem=rs,
            device_id=dev, device_id_type=pl.DeviceIdType.MESH,
        )

    def ag(d, s, k, owner):
        ref = cot.at[owner, d, pl.ds(s * rows, rows), :]
        return remote(ref, ref, ag_s.at[d * SUBS + s, k], ag_r.at[d * SUBS + s, k], {"term": ahead[d]})

    pl.semaphore_wait(barrier, n + m - 2)
    for d, s in streams:
        ag(d, s, 0, t).start()

    def forward(k):
        for d, s in streams:
            owner = term_at(pos - sign[d] * k)
            ag(d, s, k - 1, owner).wait_recv()

            @pl.when(k < n - 1)
            def _():
                ag(d, s, k, owner).start()

    z = log_ref[...]
    z = jnp.exp(z - jnp.max(z, axis=1, keepdims=True))
    gates = z / jnp.sum(z, axis=1, keepdims=True)
    gt[...] = jnp.transpose(gates)
    gbf[...] = gates.astype(BF)
    pexp[...] = jnp.dot(gbf[...], fexp_ref[...], preferred_element_type=FL)
    loads[0].wait()
    loads[1].wait()
    loads[2].wait()
    forward(1)
    pin[...] = jnp.zeros_like(pin)
    wide = 2 * half

    @pl.loop(0, n)
    def _(i):
        at = pl.ds(pl.multiple_of(i * wide, wide), wide)
        pin[...] += jnp.dot(x[:, at], fin[at, :], preferred_element_type=FL)

    hid[...] = (pin[...] * pexp[...]).astype(BF)
    ghid[...] = jnp.zeros_like(ghid)

    def add_hid(d, owner):
        at = pl.ds(pl.multiple_of(owner * wide + d * half, half), half)
        ghid[...] += jnp.dot(cot[owner, d], fout[at, :], preferred_element_type=FL)

    add_hid(0, t)
    add_hid(1, t)

    core = lax.rem(a, 2)
    xx = a // 2
    mate = {"dp": 2 * xx + 1 - core}
    across = {"dp": lax.rem(a + 2, m)}
    per = gin_ref.shape[0]
    cuts = per // half

    def part_f(w, owner, j):
        if w == 0:
            at = owner * (n // m) + j // 2
            lhs, rhs = cot[at, lax.rem(j, 2)], hid[...]
        else:
            lhs, rhs = x[:, pl.ds(pl.multiple_of(owner * per + j * half, half), half)], gpin[...]
        return lax.dot_general(lhs, rhs, FIRST, preferred_element_type=FL) * scale

    def to_mate(w, q, j):
        i = w * cuts + j
        return remote(c_send.at[q, i], c_recv.at[q, i], c_s.at[q, i], c_r.at[q, i], mate)

    def to_x(w, j):
        i = w * cuts + j
        return remote(x_send.at[i], x_recv.at[i], xs_s.at[i], xs_r.at[i], across)

    def give(w, q, j):
        chip = q * xx + (1 - q) * (1 - xx)
        c_send[q, w * cuts + j] = part_f(w, 2 * chip + 1 - core, j).astype(BF)
        to_mate(w, q, j).start()

    def pass_on(w, j):
        own = part_f(w, 2 * (1 - xx) + core, j)
        to_mate(w, 0, j).wait_recv()
        x_send[w * cuts + j] = (own + c_recv[0, w * cuts + j].astype(FL)).astype(BF)
        to_x(w, j).start()

    outs = (gout_ref, gin_ref)

    def keep(w, j):
        own = part_f(w, a, j)
        to_mate(w, 1, j).wait_recv()
        kept[w * cuts + j] = own + c_recv[1, w * cuts + j].astype(FL)

    def finish(w):
        @pl.loop(0, cuts)
        def _(j):
            to_x(w, j).wait_recv()
            at = pl.ds(pl.multiple_of(j * half, half), half)
            outs[w][at, :] = (kept[w * cuts + j] + x_recv[w * cuts + j].astype(FL)).astype(BF)

    def each(f, lo, hi):
        @pl.loop(lo, hi)
        def _(j):
            f(j)

    def place(d, k):
        at = term_at(pos - sign[d] * k)
        return at // (n // m), 2 * lax.rem(at, n // m) + d

    def hand(d, k):
        owner, j = place(d, k)

        @pl.when(lax.rem(owner, 2) != core)
        def _():
            @pl.when(owner // 2 == xx)
            def _():
                give(0, 1, j)

            @pl.when(owner // 2 != xx)
            def _():
                give(0, 0, j)

    def settle(d, k):
        owner, j = place(d, k)

        @pl.when(lax.rem(owner, 2) == core)
        def _():
            @pl.when(owner // 2 == xx)
            def _():
                keep(0, j)

            @pl.when(owner // 2 != xx)
            def _():
                pass_on(0, j)

    def add_both(k):
        for d in range(2):
            add_hid(d, term_at(pos - sign[d] * k))

    def both(f, k):
        f(0, k)
        f(1, k)

    add_both(1)
    both(hand, 0)

    @pl.loop(2, n - 1)
    def _(k):
        forward(k)
        add_both(k)
        both(hand, k - 1)
        both(settle, k - 2)

    forward(n - 1)
    add_both(n - 1)

    gh = ghid[...]
    gpin[...] = (gh * pexp[...]).astype(BF)
    ghp = gh * pin[...]
    gpexp[...] = ghp.astype(BF)

    def part_x(d, s, owner):
        at = pl.ds(pl.multiple_of(owner * wide + d * half, half), half)
        return lax.dot_general(gpin[s * rows:(s + 1) * rows, :], fin[at, :], LAST, preferred_element_type=FL)

    def rs(d, s, k):
        i = d * SUBS + s
        return remote(rs_send.at[i, k], rs_recv.at[i, k], rs_s.at[i, k], rs_r.at[i, k], {"term": ahead[d]})

    for d, s in streams:
        rs_send[d * SUBS + s, 0] = part_x(d, s, term_at(pos - sign[d])).astype(BF)
        rs(d, s, 0).start()

    def rs_step(k):
        for d, s in streams:
            i = d * SUBS + s
            own = part_x(d, s, term_at(pos - sign[d] * (k + 1)))
            rs(d, s, k - 1).wait_recv()
            rs_send[i, k] = (own + rs_recv[i, k - 1].astype(FL)).astype(BF)
            rs(d, s, k).start()

    @pl.loop(n - 2, n)
    def _(k):
        both(hand, k)
        both(settle, k - 1)

    each(lambda j: give(1, 0, j), 0, cuts // 2)
    rs_step(1)
    each(lambda j: pass_on(1, j), 0, cuts // 2)
    each(lambda j: give(1, 0, j), cuts // 2, cuts)
    both(settle, n - 1)
    each(lambda j: pass_on(1, j), cuts // 2, cuts)
    rs_step(2)

    share = gt.shape[0] // n
    row = jnp.sum(ghp * pexp[...], axis=1, keepdims=True)
    r_send[...] = jnp.transpose(jnp.broadcast_to(row, (tok, 128)))[:8]
    g_send[...] = lax.dot_general(fexp_ref[...], gpexp[...], LAST, preferred_element_type=FL).astype(BF)
    e_send[...] = (lax.dot_general(gbf[...], gpexp[...], FIRST, preferred_element_type=FL) * scale).astype(BF)
    eper = gexp_ref.shape[0]

    def g_copy(d):
        to = lax.rem(t + d, n)
        src = g_send.at[pl.ds(pl.multiple_of(to * share, share), share), :]
        return remote(src, g_recv.at[d - 1], g_s.at[d - 1], g_r.at[d - 1], {"term": to})

    def r_copy(d):
        return remote(r_send, r_recv.at[d - 1], r_s.at[d - 1], r_r.at[d - 1], {"term": lax.rem(t + d, n)})

    def e_copy(d):
        to = lax.rem(a + d, m)
        src = e_send.at[pl.ds(pl.multiple_of(to * eper, eper), eper), :]
        return remote(src, e_recv.at[d - 1], e_s.at[d - 1], e_r.at[d - 1], {"dp": to})

    for d in range(1, n):
        g_copy(d).start()
        r_copy(d).start()
    for d in range(1, m):
        e_copy(d).start()

    rs_step(3)
    each(lambda j: give(1, 1, j), 0, cuts)
    rs_step(4)
    finish(0)
    rs_step(5)
    each(lambda j: keep(1, j), 0, cuts)
    mine = pl.ds(pl.multiple_of(t * share, share), share)
    gsum = g_send[mine, :].astype(FL)
    rsum = r_send[...]
    for d in range(1, n):
        g_copy(d).wait_recv()
        r_copy(d).wait_recv()
        gsum += g_recv[d - 1].astype(FL)
        rsum += r_recv[d - 1]
    gl_ref[...] = gt[mine, :] * (gsum - rsum[:1])
    esum = e_send[pl.ds(pl.multiple_of(a * eper, eper), eper), :].astype(FL)
    for d in range(1, m):
        e_copy(d).wait_recv()
        esum += e_recv[d - 1].astype(FL)
    gexp_ref[...] = esum
    for k in range(6, n - 1):
        rs_step(k)
    finish(1)
    for d, s in streams:
        i = d * SUBS + s
        own = part_x(d, s, t)
        rs(d, s, n - 2).wait_recv()
        gx_ref[s * rows:(s + 1) * rows, d * half:(d + 1) * half] = (own + rs_recv[i, n - 2].astype(FL)).astype(BF)

    @pl.loop(0, n - 1)
    def _(k):
        for d, s in streams:
            ag(d, s, k, term_at(pos - sign[d] * k)).wait_send()
            rs(d, s, k).wait_send()

    for w in range(2):
        @pl.loop(0, cuts)
        def _(j):
            to_mate(w, 0, j).wait_send()
            to_mate(w, 1, j).wait_send()
            to_x(w, j).wait_send()

    for d in range(1, n):
        g_copy(d).wait_send()
        r_copy(d).wait_send()
    for d in range(1, m):
        e_copy(d).wait_send()


def finishing_kernel(gx, gl, gin, gout, gexp, gx_o, gl_o, gin_o, gout_o, gexp_o):
    gx_o[...] = gx[...]
    gin_o[...] = gin[...].astype(FL)
    gout_o[...] = gout[...].astype(FL)

    @pl.when(pl.program_id(0) == 0)
    def _():
        gl_o[...] = gl[...]
        gexp_o[...] = gexp[...]


def finishing(gx, gl, gin, gout, gexp):
    steps = 4
    cut = lambda v: pl.BlockSpec((v.shape[0] // steps, v.shape[1]), lambda i: (i, 0))
    full = lambda v: pl.BlockSpec(v.shape, lambda i: (0, 0))
    specs = [cut(gx), full(gl), cut(gin), cut(gout), full(gexp)]
    shape = jax.ShapeDtypeStruct
    out = pl.pallas_call(
        finishing_kernel,
        grid=(steps,),
        out_shape=(
            shape(gx.shape, BF), shape(gl.shape, FL), shape(gin.shape, FL),
            shape(gout.shape, FL), shape(gexp.shape, FL),
        ),
        in_specs=specs,
        out_specs=specs,
        compiler_params=pltpu.CompilerParams(vmem_limit_bytes=60 * 2**20),
    )(gx, gl, gin, gout, gexp)
    return out[0], out[1].T, out[2], out[3], out[4]


def fused(inputs, cotangent, logits, in_factor, out_factor, expert_factor):
    n, m = lax.axis_size("term"), lax.axis_size("dp")
    tok, wide = cotangent.shape
    width, rank = in_factor.shape
    experts = logits.shape[1]
    half, rows, per = wide // 2, tok // SUBS, width // m
    cuts = per // half
    ns = 2 * SUBS
    scale = 1.0 / math.sqrt(tok * m)
    shape = jax.ShapeDtypeStruct
    vm = pl.BlockSpec(memory_space=pltpu.VMEM)
    hbm = pl.BlockSpec(memory_space=pl.ANY)
    dma = pltpu.SemaphoreType.DMA
    out = pl.pallas_call(
        functools.partial(fused_kernel, n, m, scale),
        out_shape=(
            shape((tok, wide), BF),
            shape((experts // n, tok), FL),
            shape((per, rank), BF),
            shape((per, rank), BF),
            shape((experts // m, rank), FL),
        ),
        in_specs=[hbm, vm, vm, hbm, hbm, vm],
        out_specs=(vm,) * 5,
        scratch_shapes=[
            pltpu.VMEM((tok, width), BF),
            pltpu.VMEM((width, rank), BF),
            pltpu.VMEM((width, rank), BF),
            pltpu.VMEM((n, 2, tok, half), BF),
            pltpu.VMEM((tok, rank), FL),
            pltpu.VMEM((tok, rank), FL),
            pltpu.VMEM((tok, rank), FL),
            pltpu.VMEM((tok, rank), BF),
            pltpu.VMEM((tok, rank), BF),
            pltpu.VMEM((tok, rank), BF),
            pltpu.VMEM((experts, tok), FL),
            pltpu.VMEM((tok, experts), BF),
            pltpu.VMEM((ns, n - 1, rows, half), BF),
            pltpu.VMEM((ns, n - 1, rows, half), BF),
            pltpu.VMEM((2, 2 * cuts, half, rank), BF),
            pltpu.VMEM((2, 2 * cuts, half, rank), BF),
            pltpu.VMEM((2 * cuts, half, rank), BF),
            pltpu.VMEM((2 * cuts, half, rank), BF),
            pltpu.VMEM((2 * cuts, half, rank), FL),
            pltpu.VMEM((experts, tok), BF),
            pltpu.VMEM((n - 1, experts // n, tok), BF),
            pltpu.VMEM((8, tok), FL),
            pltpu.VMEM((n - 1, 8, tok), FL),
            pltpu.VMEM((experts, rank), BF),
            pltpu.VMEM((m - 1, experts // m, rank), BF),
            dma((3,)),
            dma((ns, n - 1)), dma((ns, n - 1)), dma((ns, n - 1)), dma((ns, n - 1)),
            dma((2, 2 * cuts)), dma((2, 2 * cuts)), dma((2 * cuts,)), dma((2 * cuts,)),
            dma((n - 1,)), dma((n - 1,)), dma((n - 1,)), dma((n - 1,)),
            dma((m - 1,)), dma((m - 1,)),
        ],
        compiler_params=pltpu.CompilerParams(
            collective_id=0, has_side_effects=True, vmem_limit_bytes=60 * 2**20
        ),
        cost_estimate=pl.CostEstimate(
            flops=10 * tok * width * rank, bytes_accessed=8 * width * rank, transcendentals=tok * experts
        ),
    )(inputs, cotangent, logits, in_factor, out_factor, expert_factor)
    return finishing(*out)


def by_collectives(inputs, cotangent, logits, in_factor, out_factor, expert_factor):
    fl = jnp.float32
    n_term = lax.axis_size("term")
    n_data = lax.axis_size("dp")
    gates = jax.nn.softmax(logits, axis=-1)
    gates_bf = gates.astype(jnp.bfloat16)
    proj_in = jnp.dot(inputs, in_factor, preferred_element_type=fl)
    proj_exp = jnp.dot(gates_bf, expert_factor, preferred_element_type=fl)
    hidden = (proj_in * proj_exp).astype(jnp.bfloat16)
    full_cotan = lax.all_gather(cotangent, "term", axis=1, tiled=True)
    grad_hid = jnp.dot(full_cotan, out_factor, preferred_element_type=fl)
    grad_pin = (grad_hid * proj_exp).astype(jnp.bfloat16)
    grad_pexp = (grad_hid * proj_in).astype(jnp.bfloat16)
    row_total = lax.psum(jnp.sum(grad_hid * proj_in * proj_exp, axis=1, keepdims=True), "term")
    contract_last = (((1,), (1,)), ((), ()))
    part_x = lax.dot_general(grad_pin, in_factor, contract_last, preferred_element_type=fl)
    part_g = lax.dot_general(grad_pexp, expert_factor, contract_last, preferred_element_type=fl)
    sum_x, grad_gate = (
        lax.psum_scatter(
            part_x.astype(jnp.bfloat16), "term", scatter_dimension=1, tiled=True
        ).astype(jnp.float32),
        lax.psum_scatter(
            part_g.astype(jnp.bfloat16), "term", scatter_dimension=1, tiled=True
        ).astype(jnp.float32),
    )
    grad_inputs = sum_x.astype(jnp.bfloat16)
    exp_local = logits.shape[1] // n_term
    gates_local = lax.dynamic_slice_in_dim(gates, lax.axis_index("term") * exp_local, exp_local, 1)
    grad_logits = gates_local * (grad_gate - row_total)
    scale = 1.0 / math.sqrt(inputs.shape[0] * n_data)
    contract_first = (((0,), (0,)), ((), ()))
    part_in = lax.dot_general(inputs, grad_pin, contract_first, preferred_element_type=fl) * scale
    part_out = (
        lax.dot_general(full_cotan, hidden, contract_first, preferred_element_type=fl) * scale
    )
    part_exp = (
        lax.dot_general(gates_bf, grad_pexp, contract_first, preferred_element_type=fl) * scale
    )
    grad_in, grad_out, grad_exp = (
        lax.psum_scatter(
            part_in.astype(jnp.bfloat16), "dp", scatter_dimension=0, tiled=True
        ).astype(jnp.float32),
        lax.psum_scatter(
            part_out.astype(jnp.bfloat16), "dp", scatter_dimension=0, tiled=True
        ).astype(jnp.float32),
        lax.psum_scatter(
            part_exp.astype(jnp.bfloat16), "dp", scatter_dimension=0, tiled=True
        ).astype(jnp.float32),
    )
    return (grad_inputs, grad_logits, grad_in, grad_out, grad_exp)


def solution(mesh):
    return jax.shard_map(
        fused if (mesh.shape["term"], mesh.shape["dp"]) == (8, 4) else by_collectives,
        mesh=mesh,
        in_specs=(
            P("dp", None),
            P("dp", "term"),
            P("dp", None),
            P(None, "term"),
            P(None, "term"),
            P(None, "term"),
        ),
        out_specs=(
            P("dp", "term"),
            P("dp", "term"),
            P("dp", "term"),
            P("dp", "term"),
            P("dp", "term"),
        ),
        check_vma=False,
    )
```
